32 devices in a mesh: grp: 2 (over x), pb: 8 (over z, y), row: 2 (over core).
Axes of the slice: x: 2, y: 2, z: 4, core: 2. Of those that a mesh axis runs over, the one named last changes fastest.
Arguments:
- record: float32 [4096, 1024], P(('grp', 'pb', 'row')), parts along dimension 0, may hold values from -12 to 12
- record_tail: float32 [254, 1024], P('grp'), parts along dimension 0, may hold values from -12 to 12
- projection: float32 [1024, 16], replicated, may hold values from -0.1875 to 0.1875
- window_start: int32 [2], P('grp'), parts along dimension 0, may hold values from 0 to 64
Outputs:
- row_profile: float32 [4096], P(('grp', 'pb', 'row')), parts along dimension 0
- col_profile: float32 [4096], P(('grp', 'pb', 'row')), parts along dimension 0
The draws below stay inside these ranges and needn't reach their ends.
There are 2 independent parts, one for each index of `grp`. The reference program is written for one: setup_inputs(seed, part) draws one part's arguments, and reference() takes and returns one part's arrays. A program takes and returns all parts, laid end to end along the dimension named above; an argument that names none is the same for every part. Nothing has to cross between parts.
All inputs are finite; a program needn't handle non-finite values.
Results may differ from the reference program's by a relative error of at most 0.0003.
Values sent between devices are 32-bit elements; how exact they have to be, the bound alone decides.
A program may use at most 64 MiB of HBM per device.

```python
import math
import jax
import jax.numpy as jnp
from jax import lax

C = 1024
K = 16
M = 64
N = 2048
HEAD = 127


def make_signal(key):
    base = jax.random.fold_in(key, 7)
    noise_key, drive_key = jax.random.split(base, 2)
    total_rows = N + HEAD
    noise = jax.random.normal(noise_key, (total_rows, C), jnp.float32)
    drive = 0.3 * jax.random.normal(drive_key, (total_rows, C), jnp.float32)

    def advance(state_now, step_input):
        state_next = 0.98 * state_now + step_input
        return (state_next, state_next)
    final_state, drift = lax.scan(advance, jnp.zeros((C,), jnp.float32), drive)
    return jnp.clip(noise + drift, -12.0, 12.0)


def draw_record(key, part):
    return make_signal(key)[:N]


def draw_record_tail(key, part):
    return make_signal(key)[N:]


def centred(stream_key, extent, scale, reach, kind=jnp.bfloat16):
    return jnp.clip(scale * jax.random.normal(stream_key, extent, jnp.float32), -reach, reach).astype(kind)


def setup_inputs(seed: int = 0, part: int = 0) -> dict:
    arg_keys = jax.random.split(jax.random.key(seed), 5)
    own_keys = jax.random.split(jax.random.fold_in(arg_keys[4], part), 5)
    return {
        "record": draw_record(jax.random.fold_in(jax.random.fold_in(arg_keys[4], part), 71), part),
        "record_tail": draw_record_tail(jax.random.fold_in(jax.random.fold_in(arg_keys[4], part), 71), part),
        "projection": centred(arg_keys[2], (C, K), C ** -0.5, 0.1875, jnp.float32),
        "window_start": jax.random.randint(own_keys[3], (1,), 0, M + 1).astype(jnp.int32),
    }


epsilon = 1e-05
ceiling = 4.0

def zscores(window, count_rows):
    hankel = jnp.stack([window[..., offset:offset + count_rows, :] for offset in range(M)], axis=-2)
    center = lax.optimization_barrier(jnp.mean(hankel, axis=-2, keepdims=True))
    spread = lax.optimization_barrier(jnp.mean(jnp.square(hankel - center), axis=-2, keepdims=True))
    scaled = (hankel - center) * lax.rsqrt(spread + epsilon) * (1.0 / math.sqrt(M * hankel.shape[-1]))
    return scaled.astype(jnp.bfloat16)

def reference(record, record_tail, projection, window_start):
    joined = jnp.concatenate([record, record_tail], axis=0)
    projected = jnp.dot(joined, projection, precision=lax.Precision.HIGHEST, preferred_element_type=jnp.float32)
    total_rows = record.shape[0]
    start_row = window_start[0].astype(jnp.int32)
    series = lax.dynamic_slice_in_dim(projected, start_row, total_rows + M - 1, 0)
    scores = zscores(series, total_rows).reshape(total_rows, -1).astype(jnp.float32)
    exclusion = M // 4
    block_rows = math.gcd(512, total_rows)
    column_index = jnp.arange(total_rows, dtype=jnp.int32)

    def one_block(block_id):
        queries = lax.dynamic_slice_in_dim(scores, block_id * block_rows, block_rows, 0)
        distance = 2.0 - 2.0 * jnp.dot(queries, scores.T, precision=lax.Precision.HIGHEST, preferred_element_type=jnp.float32)
        row_index = block_id * block_rows + jnp.arange(block_rows, dtype=jnp.int32)
        separation = column_index[None, :] - row_index[:, None]
        later_min = lax.optimization_barrier(jnp.min(jnp.where(separation > exclusion, distance, ceiling), axis=1))
        earlier_min = lax.optimization_barrier(jnp.min(jnp.where(separation < -exclusion, distance, ceiling), axis=1))
        return (later_min, earlier_min)
    later_all, earlier_all = lax.map(one_block, jnp.arange(total_rows // block_rows, dtype=jnp.int32))
    return (later_all.reshape(total_rows), earlier_all.reshape(total_rows))
```

```python
import functools
import math

import jax
import jax.numpy as jnp
from jax import lax
from jax.experimental import pallas as pl
from jax.experimental.pallas import tpu as pltpu
from jax.sharding import PartitionSpec as P

M = 64
LANES = 128
epsilon = 1e-05
MESH = pl.DeviceIdType.MESH
NT = (((1,), (1,)), ((), ()))


def kernel(
    blocks,
    row_devices,
    start_ref,
    record_hbm,
    tail_hbm,
    projection_ref,
    later_ref,
    earlier_ref,
    record_ref,
    tail_ref,
    spaced_ref,
    packed_ref,
    hankel_ref,
    own_ref,
    chunk_ref,
    load_sems,
    send_sems,
    recv_sems,
):
    rows = record_ref.shape[0]
    head_rows = tail_ref.shape[0]
    dims = projection_ref.shape[0]
    steps = LANES // dims
    packed_rows = rows // steps
    exclusion = M // 4
    pb_index = lax.axis_index("pb")
    row_index = lax.axis_index("row")
    me = pb_index * row_devices + row_index

    def place(block):
        return {"pb": lax.div(block, row_devices), "row": lax.rem(block, row_devices)}

    def peer_of(distance):
        return lax.rem(me + distance, blocks)

    def slot(block):
        return packed_ref.at[pl.ds(pl.multiple_of(block * packed_rows, packed_rows), packed_rows)]

    def block_copy(source, target, distance):
        return pltpu.make_async_remote_copy(
            src_ref=slot(source),
            dst_ref=slot(source),
            send_sem=send_sems.at[distance],
            recv_sem=recv_sems.at[source],
            device_id=place(target),
            device_id_type=MESH,
        )

    record_copy = pltpu.make_async_copy(record_hbm, record_ref, load_sems.at[0])
    record_copy.start()
    tail_copy = pltpu.make_async_copy(tail_hbm, tail_ref, load_sems.at[1])
    tail_copy.start()

    barrier = pltpu.get_barrier_semaphore()

    def greet(distance, carry):
        pl.semaphore_signal(
            barrier, inc=1, device_id=place(peer_of(distance)), device_id_type=MESH
        )
        return carry

    lax.fori_loop(1, blocks, greet, 0)

    repeated = jnp.concatenate([projection_ref[...]] * steps, axis=0)
    group = lax.broadcasted_iota(jnp.int32, (steps, LANES), 1) // dims
    row_in_group = lax.broadcasted_iota(jnp.int32, (steps, LANES), 0)
    keep = (group == row_in_group)[None]

    def pack(values):
        split = values.reshape(values.shape[0] // steps, steps, LANES)
        return jnp.sum(jnp.where(keep, split, 0.0), axis=1)

    record_copy.wait()
    projected = lax.dot_general(
        record_ref[...], repeated, NT,
        precision=lax.Precision.HIGHEST, preferred_element_type=jnp.float32,
    )
    slot(me)[...] = pack(projected)

    pl.semaphore_wait(barrier, blocks - 1)

    def send(distance, carry):
        block_copy(me, peer_of(distance), distance).start()
        return carry

    lax.fori_loop(1, blocks, send, 0)

    tail_copy.wait()
    spaced_ref[...] = jnp.zeros_like(spaced_ref)
    spaced_ref[pl.ds(0, head_rows), :] = lax.dot_general(
        tail_ref[...], repeated, NT,
        precision=lax.Precision.HIGHEST, preferred_element_type=jnp.float32,
    )
    tail_base = blocks * packed_rows
    packed_ref[pl.ds(tail_base, packed_rows), :] = pack(spaced_ref[...])
    packed_ref[pl.ds(tail_base + packed_rows, 8), :] = jnp.zeros((8, LANES), jnp.float32)

    def arrive(distance, carry):
        block_copy(peer_of(distance), me, distance).wait_recv()
        return carry

    lax.fori_loop(1, blocks, arrive, 0)

    lane = lax.broadcasted_iota(jnp.int32, (packed_rows, LANES), 1)

    def expand(block, carry):
        base = pl.multiple_of(block * packed_rows, packed_rows)
        here = packed_ref[pl.ds(base, packed_rows), :]
        after = packed_ref[pl.ds(base + 1, packed_rows), :]
        out = pl.multiple_of(block * rows, rows)
        for step in range(steps):
            if step == 0:
                moved = here
            else:
                mixed = jnp.where(lane >= step * dims, here, after)
                moved = pltpu.roll(mixed, LANES - step * dims, 1)
            hankel_ref[pl.ds(out + step, packed_rows, stride=steps), :] = moved
        return carry

    lax.fori_loop(0, blocks + 1, expand, 0, unroll=1)

    start = start_ref[0]
    turns = M // steps

    def all_steps(values):
        shift = LANES // 2
        while shift >= dims:
            values = values + pltpu.roll(values, shift, 1)
            shift //= 2
        return values

    def scores(block, out_ref, out_row):
        span = rows + M - steps
        held = hankel_ref[pl.ds(block * rows + start, span), :]
        total, reach, have = held, steps, 1
        while have < turns:
            total = total[: total.shape[0] - reach] + total[reach:]
            reach, have = reach * 2, have * 2
        center = all_steps(total[:rows]) * (1.0 / M)
        parts = [held[turn * steps : turn * steps + rows] - center for turn in range(turns)]
        square = parts[0] * parts[0]
        for part in parts[1:]:
            square = square + part * part
        spread = all_steps(square) * (1.0 / M)
        scale = lax.rsqrt(spread + epsilon) * (1.0 / math.sqrt(M * dims))
        for turn, part in enumerate(parts):
            out_ref[pl.ds(out_row, rows), pl.ds(turn * LANES, LANES)] = (part * scale).astype(
                jnp.bfloat16
            )

    scores(me, own_ref, 0)
    own = own_ref[...]
    chunk_blocks = chunk_ref.shape[0] // rows
    chunk_rows = chunk_ref.shape[0]
    offset = lax.broadcasted_iota(jnp.int32, (chunk_rows, rows), 0) - lax.broadcasted_iota(
        jnp.int32, (chunk_rows, rows), 1
    )

    def one_chunk(chunk, carry):
        later, earlier = carry
        for part in range(chunk_blocks):
            scores(chunk * chunk_blocks + part, chunk_ref, part * rows)
        product = lax.dot_general(
            chunk_ref[...], own, NT, preferred_element_type=jnp.float32
        )
        separation = offset + (chunk * chunk_rows - me * rows)
        after = jnp.where(separation > exclusion, product, -1.0)
        before = jnp.where(separation < -exclusion, product, -1.0)
        after = jnp.max(after.reshape(chunk_rows // 8, 8, rows), axis=0)
        before = jnp.max(before.reshape(chunk_rows // 8, 8, rows), axis=0)
        return jnp.maximum(later, after), jnp.maximum(earlier, before)

    low = jnp.full((8, rows), -1.0, jnp.float32)
    later, earlier = lax.fori_loop(0, blocks // chunk_blocks, one_chunk, (low, low))
    later_ref[...] = 2.0 - 2.0 * jnp.max(later, axis=0, keepdims=True)
    earlier_ref[...] = 2.0 - 2.0 * jnp.max(earlier, axis=0, keepdims=True)

    def sent(distance, carry):
        block_copy(me, peer_of(distance), distance).wait_send()
        return carry

    lax.fori_loop(1, blocks, sent, 0)


def per_device(record, record_tail, projection, window_start):
    rows, channels = record.shape
    head_rows = record_tail.shape[0]
    dims = projection.shape[1]
    row_devices = lax.axis_size("row")
    blocks = lax.axis_size("pb") * row_devices
    steps = LANES // dims
    packed_rows = rows // steps
    chunk_blocks = math.gcd(4, blocks)
    vmem = pl.BlockSpec(memory_space=pltpu.VMEM)
    hbm = pl.BlockSpec(memory_space=pl.ANY)
    f32 = jnp.float32
    later, earlier = pl.pallas_call(
        functools.partial(kernel, blocks, row_devices),
        out_shape=[jax.ShapeDtypeStruct((1, rows), f32)] * 2,
        in_specs=[pl.BlockSpec(memory_space=pltpu.SMEM), hbm, hbm, vmem],
        out_specs=[vmem, vmem],
        scratch_shapes=[
            pltpu.VMEM((rows, channels), f32),
            pltpu.VMEM((head_rows, channels), f32),
            pltpu.VMEM((rows, LANES), f32),
            pltpu.VMEM(((blocks + 1) * packed_rows + 8, LANES), f32),
            pltpu.VMEM(((blocks + 1) * rows, LANES), f32),
            pltpu.VMEM((rows, M * dims), jnp.bfloat16),
            pltpu.VMEM((chunk_blocks * rows, M * dims), jnp.bfloat16),
            pltpu.SemaphoreType.DMA((2,)),
            pltpu.SemaphoreType.DMA((blocks,)),
            pltpu.SemaphoreType.DMA((blocks,)),
        ],
        compiler_params=pltpu.CompilerParams(
            collective_id=0, has_side_effects=True, vmem_limit_bytes=40 * 1024 * 1024
        ),
    )(window_start, record, record_tail, projection.T)
    return later.reshape(rows), earlier.reshape(rows)


def solution(mesh):
    return jax.shard_map(
        per_device,
        mesh=mesh,
        in_specs=(P(("grp", "pb", "row"), None), P("grp", None), P(), P("grp")),
        out_specs=(P(("grp", "pb", "row")), P(("grp", "pb", "row"))),
        check_vma=False,
    )
```

```python
import functools
import math

import jax
import jax.numpy as jnp
from jax import lax
from jax.experimental import pallas as pl
from jax.experimental.pallas import tpu as pltpu
from jax.sharding import PartitionSpec as P

M = 64
LANES = 128
epsilon = 1e-05
MESH = pl.DeviceIdType.MESH
RECORD_COPIES = 4
NT = (((1,), (1,)), ((), ()))


def gather_kernel(
    blocks,
    row_devices,
    record_hbm,
    tail_hbm,
    projection_hbm,
    packed_ref,
    record_ref,
    tail_ref,
    projection_ref,
    spaced_ref,
    load_sems,
    send_sems,
    recv_sems,
):
    rows = record_ref.shape[0]
    head_rows = tail_ref.shape[0]
    dims = projection_ref.shape[0]
    steps = LANES // dims
    packed_rows = rows // steps
    pb_index = lax.axis_index("pb")
    row_index = lax.axis_index("row")
    me = pb_index * row_devices + row_index

    def place(block):
        return {"pb": lax.div(block, row_devices), "row": lax.rem(block, row_devices)}

    def peer_of(distance):
        return lax.rem(me + distance, blocks)

    def slot(block):
        return packed_ref.at[pl.ds(pl.multiple_of(block * packed_rows, packed_rows), packed_rows)]

    def block_copy(source, target, distance):
        return pltpu.make_async_remote_copy(
            src_ref=slot(source),
            dst_ref=slot(source),
            send_sem=send_sems.at[distance],
            recv_sem=recv_sems.at[source],
            device_id=place(target),
            device_id_type=MESH,
        )

    projection_copy = pltpu.make_async_copy(projection_hbm, projection_ref, load_sems.at[0])
    projection_copy.start()
    share = rows // RECORD_COPIES
    record_copies = [
        pltpu.make_async_copy(
            record_hbm.at[pl.ds(part * share, share)],
            record_ref.at[pl.ds(part * share, share)],
            load_sems.at[2 + part],
        )
        for part in range(RECORD_COPIES)
    ]
    for copy in record_copies:
        copy.start()
    tail_copy = pltpu.make_async_copy(tail_hbm, tail_ref, load_sems.at[1])
    tail_copy.start()

    barrier = pltpu.get_barrier_semaphore()

    def greet(distance, carry):
        pl.semaphore_signal(
            barrier, inc=1, device_id=place(peer_of(distance)), device_id_type=MESH
        )
        return carry

    lax.fori_loop(1, blocks, greet, 0)

    projection_copy.wait()
    repeated = jnp.concatenate([projection_ref[...]] * steps, axis=0)
    group = lax.broadcasted_iota(jnp.int32, (steps, LANES), 1) // dims
    row_in_group = lax.broadcasted_iota(jnp.int32, (steps, LANES), 0)
    keep = (group == row_in_group)[None]

    def pack(values):
        split = values.reshape(values.shape[0] // steps, steps, LANES)
        return jnp.sum(jnp.where(keep, split, 0.0), axis=1)

    for copy in record_copies:
        copy.wait()
    projected = lax.dot_general(
        record_ref[...], repeated, NT,
        precision=lax.Precision.HIGHEST, preferred_element_type=jnp.float32,
    )
    slot(me)[...] = pack(projected)

    pl.semaphore_wait(barrier, blocks - 1)

    def send(distance, carry):
        block_copy(me, peer_of(distance), distance).start()
        return carry

    lax.fori_loop(1, blocks, send, 0)

    tail_copy.wait()
    spaced_ref[...] = jnp.zeros_like(spaced_ref)
    spaced_ref[pl.ds(0, head_rows), :] = lax.dot_general(
        tail_ref[...], repeated, NT,
        precision=lax.Precision.HIGHEST, preferred_element_type=jnp.float32,
    )
    tail_base = blocks * packed_rows
    packed_ref[pl.ds(tail_base, packed_rows), :] = pack(spaced_ref[...])
    packed_ref[pl.ds(tail_base + packed_rows, 2 * steps), :] = jnp.zeros(
        (2 * steps, LANES), jnp.float32
    )

    def arrive(distance, carry):
        block_copy(peer_of(distance), me, distance).wait_recv()
        return carry

    lax.fori_loop(1, blocks, arrive, 0)

    def sent(distance, carry):
        block_copy(me, peer_of(distance), distance).wait_send()
        return carry

    lax.fori_loop(1, blocks, sent, 0)


def compute_kernel(
    blocks,
    row_devices,
    dims,
    start_ref,
    packed_ref,
    later_ref,
    earlier_ref,
    hankel_ref,
    center_ref,
    scale_ref,
    own_ref,
    chunk_ref,
):
    rows = own_ref.shape[0]
    steps = LANES // dims
    packed_rows = rows // steps
    tail_base = blocks * packed_rows
    exclusion = M // 4
    me = lax.axis_index("pb") * row_devices + lax.axis_index("row")

    picks = lax.broadcasted_iota(jnp.int32, (LANES, steps * LANES), 0)
    column = lax.broadcasted_iota(jnp.int32, (LANES, steps * LANES), 1)
    pick = (picks == column // LANES * dims + column % dims).astype(jnp.float32)
    pick = pick.astype(jnp.bfloat16)
    pick = jnp.concatenate([pick, pick, pick], axis=0)

    def later_steps(values, by):
        size = values.shape[0]
        if by >= steps:
            return pltpu.roll(values, size - by // steps, 0)
        lane = lax.broadcasted_iota(jnp.int32, values.shape, 1)
        mixed = jnp.where(lane >= by * dims, values, pltpu.roll(values, size - 1, 0))
        return pltpu.roll(mixed, LANES - by * dims, 1)

    def three_terms(values):
        high = values.astype(jnp.bfloat16)
        rest = values - high.astype(jnp.float32)
        middle = rest.astype(jnp.bfloat16)
        low = (rest - middle.astype(jnp.float32)).astype(jnp.bfloat16)
        return jnp.concatenate([high, middle, low], axis=1)

    def expand(base, count):
        held = packed_ref[pl.ds(base, count + 2 * steps), :]
        out = base * steps
        for step in range(steps):
            moved = held if step == 0 else later_steps(held, step)
            hankel_ref[pl.ds(out + step, count, stride=steps), :] = moved[:count]
        total = held
        square = jnp.zeros_like(held)
        have = 1
        while have < M:
            next_total = later_steps(total, have)
            if have > 1:
                square = square + later_steps(square, have)
            gap = total - next_total
            square = square + gap * gap * (0.5 / have)
            total = total + next_total
            have *= 2
        center = total[:count] * (1.0 / M)
        scale = lax.rsqrt(square[:count] * (1.0 / M) + epsilon) * (1.0 / math.sqrt(M * dims))
        for values, ref in ((center, center_ref), (scale, scale_ref)):
            spread_out = jnp.dot(
                three_terms(values), pick, preferred_element_type=jnp.float32
            )
            for step in range(steps):
                ref[pl.ds(out + step, count, stride=steps), :] = spread_out[
                    :, step * LANES : (step + 1) * LANES
                ]

    group_blocks = math.gcd(16, blocks)
    group_rows = group_blocks * packed_rows

    def expand_group(index, carry):
        expand(pl.multiple_of(index * group_rows, group_rows), group_rows)
        return carry

    if group_blocks == blocks:
        expand(0, tail_base + packed_rows)
    else:
        lax.fori_loop(0, blocks // group_blocks, expand_group, 0)
        expand(tail_base, packed_rows)

    start = start_ref[0]
    turns = M // steps
    piece = min(64, rows)

    def scores(first, out_ref, out_row):
        held = hankel_ref[pl.ds(first + start, piece + M - steps), :]
        center = center_ref[pl.ds(first + start, piece), :]
        scale = scale_ref[pl.ds(first + start, piece), :]
        for turn in range(turns):
            part = (held[turn * steps : turn * steps + piece] - center) * scale
            out_ref[pl.ds(out_row, piece), pl.ds(turn * LANES, LANES)] = part.astype(
                jnp.bfloat16
            )

    for part in range(rows // piece):
        scores(me * rows + part * piece, own_ref, part * piece)
    own = own_ref[...]
    chunk_rows = chunk_ref.shape[0]
    half = chunk_rows // 2
    offset = lax.broadcasted_iota(jnp.int32, (half, rows), 0) - lax.broadcasted_iota(
        jnp.int32, (half, rows), 1
    )

    def one_chunk(chunk, carry):
        later, earlier = carry
        for side in range(2):
            for part in range(half // piece):
                row = side * half + part * piece
                scores(chunk * chunk_rows + row, chunk_ref, row)
            product = lax.dot_general(
                chunk_ref[pl.ds(side * half, half), :], own, NT,
                preferred_element_type=jnp.float32,
            )
            separation = offset + (chunk * chunk_rows + side * half - me * rows)
            after = jnp.where(separation > exclusion, product, -1.0)
            before = jnp.where(separation < -exclusion, product, -1.0)
            after = jnp.max(after.reshape(half // 8, 8, rows), axis=0)
            before = jnp.max(before.reshape(half // 8, 8, rows), axis=0)
            later, earlier = jnp.maximum(later, after), jnp.maximum(earlier, before)
        return later, earlier

    chunk_blocks = chunk_rows // rows
    low = jnp.full((8, rows), -1.0, jnp.float32)
    later, earlier = lax.fori_loop(0, blocks // chunk_blocks, one_chunk, (low, low))
    later_ref[...] = 2.0 - 2.0 * jnp.max(later, axis=0, keepdims=True)
    earlier_ref[...] = 2.0 - 2.0 * jnp.max(earlier, axis=0, keepdims=True)


def per_device(record, record_tail, projection, window_start):
    rows, channels = record.shape
    head_rows = record_tail.shape[0]
    dims = projection.shape[1]
    row_devices = lax.axis_size("row")
    blocks = lax.axis_size("pb") * row_devices
    steps = LANES // dims
    packed_rows = rows // steps
    chunk_blocks = math.gcd(4, blocks)
    vmem = pl.BlockSpec(memory_space=pltpu.VMEM)
    hbm = pl.BlockSpec(memory_space=pltpu.HBM)
    f32 = jnp.float32
    packed = pl.pallas_call(
        functools.partial(gather_kernel, blocks, row_devices),
        out_shape=jax.ShapeDtypeStruct(((blocks + 1) * packed_rows + 2 * steps, LANES), f32),
        in_specs=[hbm, hbm, hbm],
        out_specs=vmem,
        scratch_shapes=[
            pltpu.VMEM((rows, channels), f32),
            pltpu.VMEM((head_rows, channels), f32),
            pltpu.VMEM((dims, channels), f32),
            pltpu.VMEM((rows, LANES), f32),
            pltpu.SemaphoreType.DMA((2 + RECORD_COPIES,)),
            pltpu.SemaphoreType.DMA((blocks,)),
            pltpu.SemaphoreType.DMA((blocks,)),
        ],
        compiler_params=pltpu.CompilerParams(
            collective_id=0, has_side_effects=True, vmem_limit_bytes=62 * 1024 * 1024
        ),
    )(record, record_tail, projection.T)
    later, earlier = pl.pallas_call(
        functools.partial(compute_kernel, blocks, row_devices, dims),
        out_shape=[jax.ShapeDtypeStruct((1, rows), f32)] * 2,
        in_specs=[pl.BlockSpec(memory_space=pltpu.SMEM), vmem],
        out_specs=[vmem, vmem],
        scratch_shapes=[pltpu.VMEM(((blocks + 1) * rows, LANES), f32)] * 3
        + [
            pltpu.VMEM((rows, M * dims), jnp.bfloat16),
            pltpu.VMEM((chunk_blocks * rows, M * dims), jnp.bfloat16),
        ],
        compiler_params=pltpu.CompilerParams(vmem_limit_bytes=48 * 1024 * 1024),
    )(window_start, packed)
    return later.reshape(rows), earlier.reshape(rows)


def solution(mesh):
    return jax.shard_map(
        per_device,
        mesh=mesh,
        in_specs=(P(("grp", "pb", "row"), None), P("grp", None), P(), P("grp")),
        out_specs=(P(("grp", "pb", "row")), P(("grp", "pb", "row"))),
        check_vma=False,
    )
```

```python
import functools
import math

import jax
import jax.numpy as jnp
from jax import lax
from jax.experimental import pallas as pl
from jax.experimental.pallas import tpu as pltpu
from jax.sharding import PartitionSpec as P

M = 64
LANES = 128
epsilon = 1e-05
MESH = pl.DeviceIdType.MESH
RECORD_COPIES = 4
NT = (((1,), (1,)), ((), ()))


def kernel(
    blocks,
    row_devices,
    start_ref,
    record_hbm,
    tail_hbm,
    projection_hbm,
    best_ref,
    record_ref,
    tail_ref,
    projection_ref,
    spaced_ref,
    packed_ref,
    hankel_ref,
    center_ref,
    scale_ref,
    own_ref,
    chunk_ref,
    pick_ref,
    load_sems,
    send_sems,
    recv_sems,
):
    rows = record_ref.shape[0]
    head_rows = tail_ref.shape[0]
    dims = projection_ref.shape[0]
    steps = LANES // dims
    packed_rows = rows // steps
    exclusion = M // 4
    pb_index = lax.axis_index("pb")
    row_index = lax.axis_index("row")
    me = pb_index * row_devices + row_index
    unroll = blocks - 1 if blocks <= 16 else 1

    def place(block):
        return {"pb": lax.div(block, row_devices), "row": lax.rem(block, row_devices)}

    def peer_of(distance):
        return lax.rem(me + distance, blocks)

    def slot(block):
        return packed_ref.at[pl.ds(pl.multiple_of(block * packed_rows, packed_rows), packed_rows)]

    def block_copy(source, target, distance):
        return pltpu.make_async_remote_copy(
            src_ref=slot(source),
            dst_ref=slot(source),
            send_sem=send_sems.at[distance],
            recv_sem=recv_sems.at[source],
            device_id=place(target),
            device_id_type=MESH,
        )

    projection_copy = pltpu.make_async_copy(projection_hbm, projection_ref, load_sems.at[0])
    projection_copy.start()
    share = rows // RECORD_COPIES
    record_copies = [
        pltpu.make_async_copy(
            record_hbm.at[pl.ds(part * share, share)],
            record_ref.at[pl.ds(part * share, share)],
            load_sems.at[2 + part],
        )
        for part in range(RECORD_COPIES)
    ]
    for copy in record_copies:
        copy.start()
    tail_copy = pltpu.make_async_copy(tail_hbm, tail_ref, load_sems.at[1])
    tail_copy.start()

    barrier = pltpu.get_barrier_semaphore()

    def greet(distance, carry):
        pl.semaphore_signal(
            barrier, inc=1, device_id=place(peer_of(distance)), device_id_type=MESH
        )
        return carry

    lax.fori_loop(1, blocks, greet, 0, unroll=unroll)

    picks = lax.broadcasted_iota(jnp.int32, (LANES, steps * LANES), 0)
    column = lax.broadcasted_iota(jnp.int32, (LANES, steps * LANES), 1)
    pick = (picks == column // LANES * dims + column % dims).astype(jnp.float32)
    pick = pick.astype(jnp.bfloat16)
    pick = jnp.concatenate([pick, pick, pick], axis=0)
    pick_ref[...] = pick

    projection_copy.wait()
    repeated = jnp.concatenate([projection_ref[...]] * steps, axis=0)
    group = lax.broadcasted_iota(jnp.int32, (steps, LANES), 1) // dims
    row_in_group = lax.broadcasted_iota(jnp.int32, (steps, LANES), 0)
    keep = (group == row_in_group)[None]

    def pack(values):
        split = values.reshape(values.shape[0] // steps, steps, LANES)
        return jnp.sum(jnp.where(keep, split, 0.0), axis=1)

    for copy in record_copies:
        copy.wait()
    projected = lax.dot_general(
        record_ref[...], repeated, NT,
        precision=lax.Precision.HIGHEST, preferred_element_type=jnp.float32,
    )
    slot(me)[...] = pack(projected)

    pl.semaphore_wait(barrier, blocks - 1)

    def send(distance, carry):
        block_copy(me, peer_of(distance), distance).start()
        return carry

    lax.fori_loop(1, blocks, send, 0, unroll=unroll)

    tail_copy.wait()
    spaced_ref[...] = jnp.zeros_like(spaced_ref)
    spaced_ref[pl.ds(0, head_rows), :] = lax.dot_general(
        tail_ref[...], repeated, NT,
        precision=lax.Precision.HIGHEST, preferred_element_type=jnp.float32,
    )
    tail_base = blocks * packed_rows
    packed_ref[pl.ds(tail_base, packed_rows), :] = pack(spaced_ref[...])
    packed_ref[pl.ds(tail_base + packed_rows, 2 * steps), :] = jnp.zeros(
        (2 * steps, LANES), jnp.float32
    )

    def arrive(distance, carry):
        block_copy(peer_of(distance), me, distance).wait_recv()
        return carry

    lax.fori_loop(1, blocks, arrive, 0, unroll=unroll)

    def later_steps(values, by):
        size = values.shape[0]
        if by >= steps:
            return pltpu.roll(values, size - by // steps, 0)
        lane = lax.broadcasted_iota(jnp.int32, values.shape, 1)
        mixed = jnp.where(lane >= by * dims, values, pltpu.roll(values, size - 1, 0))
        return pltpu.roll(mixed, LANES - by * dims, 1)

    def three_terms(values):
        high = values.astype(jnp.bfloat16)
        rest = values - high.astype(jnp.float32)
        middle = rest.astype(jnp.bfloat16)
        low = (rest - middle.astype(jnp.float32)).astype(jnp.bfloat16)
        return jnp.concatenate([high, middle, low], axis=1)

    def expand(base, count):
        held = packed_ref[pl.ds(base, count + 2 * steps), :]
        out = base * steps
        for step in range(steps):
            moved = held if step == 0 else later_steps(held, step)
            hankel_ref[pl.ds(out + step, count, stride=steps), :] = moved[:count]
        total = held
        square = jnp.zeros_like(held)
        have = 1
        while have < M:
            next_total = later_steps(total, have)
            if have > 1:
                square = square + later_steps(square, have)
            gap = total - next_total
            square = square + gap * gap * (0.5 / have)
            total = total + next_total
            have *= 2
        center = total[:count] * (1.0 / M)
        scale = lax.rsqrt(square[:count] * (1.0 / M) + epsilon) * (1.0 / math.sqrt(M * dims))
        for values, ref in ((center, center_ref), (scale, scale_ref)):
            spread_out = jnp.dot(
                three_terms(values), pick_ref[...], preferred_element_type=jnp.float32
            )
            for step in range(steps):
                ref[pl.ds(out + step, count, stride=steps), :] = spread_out[
                    :, step * LANES : (step + 1) * LANES
                ]

    group_blocks = math.gcd(16, blocks)
    group_rows = group_blocks * packed_rows

    def expand_group(index, carry):
        expand(pl.multiple_of(index * group_rows, group_rows), group_rows)
        return carry

    if group_blocks == blocks:
        expand(0, tail_base + packed_rows)
    else:
        lax.fori_loop(0, blocks // group_blocks, expand_group, 0)
        expand(tail_base, packed_rows)

    start = start_ref[0]
    turns = M // steps
    piece = min(64, rows)

    def scores(first, out_ref, out_row):
        held = hankel_ref[pl.ds(first + start, piece + M - steps), :]
        center = center_ref[pl.ds(first + start, piece), :]
        scale = scale_ref[pl.ds(first + start, piece), :]
        for turn in range(turns):
            part = (held[turn * steps : turn * steps + piece] - center) * scale
            out_ref[pl.ds(out_row, piece), pl.ds(turn * LANES, LANES)] = part.astype(
                jnp.bfloat16
            )

    for part in range(rows // piece):
        scores(me * rows + part * piece, own_ref, part * piece)
    own = own_ref[...]
    chunk_rows = chunk_ref.shape[0]
    half = min(2 * rows, chunk_rows)
    offset = lax.broadcasted_iota(jnp.int32, (half, rows), 0) - lax.broadcasted_iota(
        jnp.int32, (half, rows), 1
    )

    def one_chunk(chunk, carry):
        later, earlier = carry
        for side in range(chunk_rows // half):
            for part in range(half // piece):
                row = side * half + part * piece
                scores(chunk * chunk_rows + row, chunk_ref, row)
            product = lax.dot_general(
                chunk_ref[pl.ds(side * half, half), :], own, NT,
                preferred_element_type=jnp.float32,
            )
            separation = offset + (chunk * chunk_rows + side * half - me * rows)
            after = jnp.where(separation > exclusion, product, -1.0)
            before = jnp.where(separation < -exclusion, product, -1.0)
            after = jnp.max(after.reshape(half // 8, 8, rows), axis=0)
            before = jnp.max(before.reshape(half // 8, 8, rows), axis=0)
            later, earlier = jnp.maximum(later, after), jnp.maximum(earlier, before)
        return later, earlier

    chunk_blocks = chunk_rows // rows
    low = jnp.full((8, rows), -1.0, jnp.float32)
    later, earlier = lax.fori_loop(0, blocks // chunk_blocks, one_chunk, (low, low))
    best_ref[pl.ds(0, 1), :] = 2.0 - 2.0 * jnp.max(later, axis=0, keepdims=True)
    best_ref[pl.ds(1, 1), :] = 2.0 - 2.0 * jnp.max(earlier, axis=0, keepdims=True)

    def sent(distance, carry):
        block_copy(me, peer_of(distance), distance).wait_send()
        return carry

    lax.fori_loop(1, blocks, sent, 0, unroll=unroll)


def split_kernel(best_ref, later_ref, earlier_ref, sems):
    copies = [
        pltpu.make_async_copy(best_ref.at[pl.ds(row, 1)], ref, sems.at[row])
        for row, ref in enumerate((later_ref, earlier_ref))
    ]
    for copy in copies:
        copy.start()
    for copy in copies:
        copy.wait()


def per_device(record, record_tail, projection, window_start):
    rows, channels = record.shape
    head_rows = record_tail.shape[0]
    dims = projection.shape[1]
    row_devices = lax.axis_size("row")
    blocks = lax.axis_size("pb") * row_devices
    steps = LANES // dims
    packed_rows = rows // steps
    chunk_blocks = math.gcd(16, blocks)
    vmem = pl.BlockSpec(memory_space=pltpu.VMEM)
    hbm = pl.BlockSpec(memory_space=pltpu.HBM)
    f32 = jnp.float32
    best = pl.pallas_call(
        functools.partial(kernel, blocks, row_devices),
        out_shape=jax.ShapeDtypeStruct((2, rows), f32),
        in_specs=[pl.BlockSpec(memory_space=pltpu.SMEM), hbm, hbm, hbm],
        out_specs=vmem,
        scratch_shapes=[
            pltpu.VMEM((rows, channels), f32),
            pltpu.VMEM((head_rows, channels), f32),
            pltpu.VMEM((dims, channels), f32),
            pltpu.VMEM((rows, LANES), f32),
            pltpu.VMEM(((blocks + 1) * packed_rows + 2 * steps, LANES), f32),
            pltpu.VMEM(((blocks + 1) * rows, LANES), f32),
            pltpu.VMEM(((blocks + 1) * rows, LANES), f32),
            pltpu.VMEM(((blocks + 1) * rows, LANES), f32),
            pltpu.VMEM((rows, M * dims), jnp.bfloat16),
            pltpu.VMEM((chunk_blocks * rows, M * dims), jnp.bfloat16),
            pltpu.VMEM((3 * LANES, steps * LANES), jnp.bfloat16),
            pltpu.SemaphoreType.DMA((2 + RECORD_COPIES,)),
            pltpu.SemaphoreType.DMA((blocks,)),
            pltpu.SemaphoreType.DMA((blocks,)),
        ],
        compiler_params=pltpu.CompilerParams(
            collective_id=0, has_side_effects=True, vmem_limit_bytes=62 * 1024 * 1024
        ),
    )(window_start, record, record_tail, projection.T)
    later, earlier = pl.pallas_call(
        split_kernel,
        out_shape=[jax.ShapeDtypeStruct((1, rows), f32)] * 2,
        in_specs=[hbm],
        out_specs=[hbm, hbm],
        scratch_shapes=[pltpu.SemaphoreType.DMA((2,))],
        compiler_params=pltpu.CompilerParams(vmem_limit_bytes=62 * 1024 * 1024),
    )(best)
    return later.reshape(rows), earlier.reshape(rows)


def solution(mesh):
    return jax.shard_map(
        per_device,
        mesh=mesh,
        in_specs=(P(("grp", "pb", "row"), None), P("grp", None), P(), P("grp")),
        out_specs=(P(("grp", "pb", "row")), P(("grp", "pb", "row"))),
        check_vma=False,
    )
```

```python
import functools
import math

import jax
import jax.numpy as jnp
from jax import lax
from jax.experimental import pallas as pl
from jax.experimental.pallas import tpu as pltpu
from jax.sharding import PartitionSpec as P

M = 64
LANES = 128
epsilon = 1e-05
MESH = pl.DeviceIdType.MESH
RECORD_COPIES = 8
NT = (((1,), (1,)), ((), ()))


def kernel(
    blocks,
    row_devices,
    start_ref,
    record_hbm,
    tail_hbm,
    projection_hbm,
    best_ref,
    record_ref,
    tail_ref,
    projection_ref,
    spaced_ref,
    packed_ref,
    hankel_ref,
    center_ref,
    scale_ref,
    own_ref,
    chunk_ref,
    pick_ref,
    load_sems,
    send_sems,
    recv_sems,
):
    rows = record_ref.shape[0]
    head_rows = tail_ref.shape[0]
    dims = projection_ref.shape[0]
    steps = LANES // dims
    packed_rows = rows // steps
    exclusion = M // 4
    pb_index = lax.axis_index("pb")
    row_index = lax.axis_index("row")
    me = pb_index * row_devices + row_index
    unroll = blocks - 1 if blocks <= 16 else 1

    def place(block):
        return {"pb": lax.div(block, row_devices), "row": lax.rem(block, row_devices)}

    def peer_of(distance):
        return lax.rem(me + distance, blocks)

    def slot(block):
        return packed_ref.at[pl.ds(pl.multiple_of(block * packed_rows, packed_rows), packed_rows)]

    def block_copy(source, target, distance):
        return pltpu.make_async_remote_copy(
            src_ref=slot(source),
            dst_ref=slot(source),
            send_sem=send_sems.at[distance],
            recv_sem=recv_sems.at[source],
            device_id=place(target),
            device_id_type=MESH,
        )

    projection_copy = pltpu.make_async_copy(projection_hbm, projection_ref, load_sems.at[0])
    projection_copy.start()
    share = rows // RECORD_COPIES
    record_copies = [
        pltpu.make_async_copy(
            record_hbm.at[pl.ds(part * share, share)],
            record_ref.at[pl.ds(part * share, share)],
            load_sems.at[2 + part],
        )
        for part in range(RECORD_COPIES)
    ]
    for copy in record_copies:
        copy.start()
    tail_copy = pltpu.make_async_copy(tail_hbm, tail_ref, load_sems.at[1])
    tail_copy.start()

    barrier = pltpu.get_barrier_semaphore()

    def greet(distance, carry):
        pl.semaphore_signal(
            barrier, inc=1, device_id=place(peer_of(distance)), device_id_type=MESH
        )
        return carry

    lax.fori_loop(1, blocks, greet, 0, unroll=unroll)

    picks = lax.broadcasted_iota(jnp.int32, (LANES, steps * LANES), 0)
    column = lax.broadcasted_iota(jnp.int32, (LANES, steps * LANES), 1)
    pick = (picks == column // LANES * dims + column % dims).astype(jnp.float32)
    pick = pick.astype(jnp.bfloat16)
    pick = jnp.concatenate([pick, pick, pick], axis=0)
    pick_ref[...] = pick

    projection_copy.wait()
    repeated = jnp.concatenate([projection_ref[...]] * steps, axis=0)
    group = lax.broadcasted_iota(jnp.int32, (steps, LANES), 1) // dims
    row_in_group = lax.broadcasted_iota(jnp.int32, (steps, LANES), 0)
    keep = (group == row_in_group)[None]

    def pack(values):
        split = values.reshape(values.shape[0] // steps, steps, LANES)
        return jnp.sum(jnp.where(keep, split, 0.0), axis=1)

    for copy in record_copies:
        copy.wait()
    projected = lax.dot_general(
        record_ref[...], repeated, NT,
        precision=lax.Precision.HIGHEST, preferred_element_type=jnp.float32,
    )
    slot(me)[...] = pack(projected)

    pl.semaphore_wait(barrier, blocks - 1)

    def send(distance, carry):
        block_copy(me, peer_of(distance), distance).start()
        return carry

    lax.fori_loop(1, blocks, send, 0, unroll=unroll)

    tail_copy.wait()
    spaced_ref[...] = jnp.zeros_like(spaced_ref)
    spaced_ref[pl.ds(0, head_rows), :] = lax.dot_general(
        tail_ref[...], repeated, NT,
        precision=lax.Precision.HIGHEST, preferred_element_type=jnp.float32,
    )
    tail_base = blocks * packed_rows
    packed_ref[pl.ds(tail_base, packed_rows), :] = pack(spaced_ref[...])
    packed_ref[pl.ds(tail_base + packed_rows, 2 * steps), :] = jnp.zeros(
        (2 * steps, LANES), jnp.float32
    )

    def arrive(distance, carry):
        block_copy(peer_of(distance), me, distance).wait_recv()
        return carry

    lax.fori_loop(1, blocks, arrive, 0, unroll=unroll)

    def later_steps(values, by):
        size = values.shape[0]
        if by >= steps:
            return pltpu.roll(values, size - by // steps, 0)
        lane = lax.broadcasted_iota(jnp.int32, values.shape, 1)
        mixed = jnp.where(lane >= by * dims, values, pltpu.roll(values, size - 1, 0))
        return pltpu.roll(mixed, LANES - by * dims, 1)

    def three_terms(values):
        high = values.astype(jnp.bfloat16)
        rest = values - high.astype(jnp.float32)
        middle = rest.astype(jnp.bfloat16)
        low = (rest - middle.astype(jnp.float32)).astype(jnp.bfloat16)
        return jnp.concatenate([high, middle, low], axis=1)

    def expand(base, count):
        held = packed_ref[pl.ds(base, count + 2 * steps), :]
        out = base * steps
        for step in range(steps):
            moved = held if step == 0 else later_steps(held, step)
            hankel_ref[pl.ds(out + step, count, stride=steps), :] = moved[:count]
        total = held
        square = jnp.zeros_like(held)
        have = 1
        while have < M:
            next_total = later_steps(total, have)
            if have > 1:
                square = square + later_steps(square, have)
            gap = total - next_total
            square = square + gap * gap * (0.5 / have)
            total = total + next_total
            have *= 2
        center = total[:count] * (1.0 / M)
        scale = lax.rsqrt(square[:count] * (1.0 / M) + epsilon) * (1.0 / math.sqrt(M * dims))
        for values, ref in ((center, center_ref), (scale, scale_ref)):
            spread_out = jnp.dot(
                three_terms(values), pick_ref[...], preferred_element_type=jnp.float32
            )
            for step in range(steps):
                ref[pl.ds(out + step, count, stride=steps), :] = spread_out[
                    :, step * LANES : (step + 1) * LANES
                ]

    group_blocks = math.gcd(16, blocks)
    group_rows = group_blocks * packed_rows

    def expand_group(index, carry):
        expand(pl.multiple_of(index * group_rows, group_rows), group_rows)
        return carry

    if group_blocks == blocks:
        expand(0, tail_base + packed_rows)
    else:
        lax.fori_loop(0, blocks // group_blocks, expand_group, 0)
        expand(tail_base, packed_rows)

    start = start_ref[0]
    turns = M // steps
    piece = min(64, rows)

    def scores(first, out_ref, out_row):
        held = hankel_ref[pl.ds(first + start, piece + M - steps), :]
        center = center_ref[pl.ds(first + start, piece), :]
        scale = scale_ref[pl.ds(first + start, piece), :]
        for turn in range(turns):
            part = (held[turn * steps : turn * steps + piece] - center) * scale
            out_ref[pl.ds(out_row, piece), pl.ds(turn * LANES, LANES)] = part.astype(
                jnp.bfloat16
            )

    for part in range(rows // piece):
        scores(me * rows + part * piece, own_ref, part * piece)
    own = own_ref[...]
    chunk_rows = chunk_ref.shape[0]
    half = min(2 * rows, chunk_rows)
    offset = lax.broadcasted_iota(jnp.int32, (half, rows), 0) - lax.broadcasted_iota(
        jnp.int32, (half, rows), 1
    )

    def one_chunk(chunk, carry):
        later, earlier = carry
        for side in range(chunk_rows // half):
            for part in range(half // piece):
                row = side * half + part * piece
                scores(chunk * chunk_rows + row, chunk_ref, row)
            product = lax.dot_general(
                chunk_ref[pl.ds(side * half, half), :], own, NT,
                preferred_element_type=jnp.float32,
            )
            origin = me * rows - chunk * chunk_rows - side * half
            after = jnp.where(offset > origin + exclusion, product, -1.0)
            before = jnp.where(offset < origin - exclusion, product, -1.0)
            after = jnp.max(after.reshape(half // 8, 8, rows), axis=0)
            before = jnp.max(before.reshape(half // 8, 8, rows), axis=0)
            later, earlier = jnp.maximum(later, after), jnp.maximum(earlier, before)
        return later, earlier

    chunk_blocks = chunk_rows // rows
    low = jnp.full((8, rows), -1.0, jnp.float32)
    later, earlier = lax.fori_loop(0, blocks // chunk_blocks, one_chunk, (low, low))
    best_ref[pl.ds(0, 1), :] = 2.0 - 2.0 * jnp.max(later, axis=0, keepdims=True)
    best_ref[pl.ds(1, 1), :] = 2.0 - 2.0 * jnp.max(earlier, axis=0, keepdims=True)

    def sent(distance, carry):
        block_copy(me, peer_of(distance), distance).wait_send()
        return carry

    lax.fori_loop(1, blocks, sent, 0, unroll=unroll)


def split_kernel(best_ref, later_ref, earlier_ref, sems):
    copies = [
        pltpu.make_async_copy(best_ref.at[pl.ds(row, 1)], ref, sems.at[row])
        for row, ref in enumerate((later_ref, earlier_ref))
    ]
    for copy in copies:
        copy.start()
    for copy in copies:
        copy.wait()


def per_device(record, record_tail, projection, window_start):
    rows, channels = record.shape
    head_rows = record_tail.shape[0]
    dims = projection.shape[1]
    row_devices = lax.axis_size("row")
    blocks = lax.axis_size("pb") * row_devices
    steps = LANES // dims
    packed_rows = rows // steps
    chunk_blocks = math.gcd(16, blocks)
    vmem = pl.BlockSpec(memory_space=pltpu.VMEM)
    hbm = pl.BlockSpec(memory_space=pltpu.HBM)
    f32 = jnp.float32
    best = pl.pallas_call(
        functools.partial(kernel, blocks, row_devices),
        out_shape=jax.ShapeDtypeStruct((2, rows), f32),
        in_specs=[pl.BlockSpec(memory_space=pltpu.SMEM), hbm, hbm, hbm],
        out_specs=vmem,
        scratch_shapes=[
            pltpu.VMEM((rows, channels), f32),
            pltpu.VMEM((head_rows, channels), f32),
            pltpu.VMEM((dims, channels), f32),
            pltpu.VMEM((rows, LANES), f32),
            pltpu.VMEM(((blocks + 1) * packed_rows + 2 * steps, LANES), f32),
            pltpu.VMEM(((blocks + 1) * rows, LANES), f32),
            pltpu.VMEM(((blocks + 1) * rows, LANES), f32),
            pltpu.VMEM(((blocks + 1) * rows, LANES), f32),
            pltpu.VMEM((rows, M * dims), jnp.bfloat16),
            pltpu.VMEM((chunk_blocks * rows, M * dims), jnp.bfloat16),
            pltpu.VMEM((3 * LANES, steps * LANES), jnp.bfloat16),
            pltpu.SemaphoreType.DMA((2 + RECORD_COPIES,)),
            pltpu.SemaphoreType.DMA((blocks,)),
            pltpu.SemaphoreType.DMA((blocks,)),
        ],
        compiler_params=pltpu.CompilerParams(
            collective_id=0, has_side_effects=True, vmem_limit_bytes=62 * 1024 * 1024
        ),
    )(window_start, record, record_tail, projection.T)
    later, earlier = pl.pallas_call(
        split_kernel,
        out_shape=[jax.ShapeDtypeStruct((1, rows), f32)] * 2,
        in_specs=[hbm],
        out_specs=[hbm, hbm],
        scratch_shapes=[pltpu.SemaphoreType.DMA((2,))],
        compiler_params=pltpu.CompilerParams(vmem_limit_bytes=62 * 1024 * 1024),
    )(best)
    return later.reshape(rows), earlier.reshape(rows)


def solution(mesh):
    return jax.shard_map(
        per_device,
        mesh=mesh,
        in_specs=(P(("grp", "pb", "row"), None), P("grp", None), P(), P("grp")),
        out_specs=(P(("grp", "pb", "row")), P(("grp", "pb", "row"))),
        check_vma=False,
    )
```
